32 devices in a mesh: ctx: 8 (over z, y), head: 4 (over x, core).
Axes of the slice: x: 2, y: 2, z: 4, core: 2. Of those that a mesh axis runs over, the one named last changes fastest.
Arguments:
- queries: bfloat16 [8192, 4096], P('ctx', 'head'), may hold values from -6 to 6
- keys: bfloat16 [8192, 1024], P('ctx', 'head'), may hold values from -6 to 6
- values: bfloat16 [8192, 1024], P('ctx', 'head'), may hold values from -6 to 6
- block_masks: int32 [32, 64], P('head', 'ctx'), may hold values from 0 to 63
- residual: bfloat16 [8192, 4096], P(('ctx', 'head')), may hold values from -1.5 to 1.5
- norm_gain: bfloat16 [4096], replicated, may hold values from 0.099609375 to 1.8984375
Outputs:
- stream: bfloat16 [8192, 4096], P(('ctx', 'head'))
- normed: bfloat16 [8192, 4096], P(('ctx', 'head'))
The draws below stay inside these ranges and needn't reach their ends.
Inputs may be any that keep to these rules, and one draw needn't show every extreme that they name: Bit b of block_masks[h, i] says whether query block i of head h attends to block i XOR 2^b; it is read only where that block comes earlier, and bits from 6 up are zero.
All inputs are finite; a program needn't handle non-finite values.
Results may differ from the reference program's by a relative error of at most 0.0052.
Values may be sent and summed in bfloat16 or wider, within the bound.
A program may use at most 64 MiB of HBM per device.

```python
import jax
import jax.numpy as jnp
from jax import lax

QH = 32
KVH = 8
DH = 128
BLOCK = 128
D = 4096
LEVELS = 6
SEQ = 8192
NB = 64


def drawn_pair(key):
    base = jax.random.fold_in(key, 7)
    key_query, key_key = jax.random.split(base, 2)
    queries = jnp.clip(jax.random.normal(key_query, (SEQ, QH * DH), jnp.float32), -6.0, 6.0)
    keys = jnp.clip(jax.random.normal(key_key, (SEQ, KVH * DH), jnp.float32), -6.0, 6.0)
    return (queries, keys)


def draw_queries(key, part):
    queries, _ = drawn_pair(key)
    return queries.astype(jnp.bfloat16)


def draw_keys(key, part):
    _, keys = drawn_pair(key)
    return keys.astype(jnp.bfloat16)


def touch_ends(drawn, rng, least, top_value):
    shape = drawn.shape
    place = [jax.random.randint(jax.random.fold_in(rng, axis), (), 0, shape[axis]) for axis in range(len(shape))]
    drawn = drawn.at[tuple(place)].set(least)
    longest = shape.index(max(shape))
    place[longest] = (place[longest] + 1) % shape[longest]
    return drawn.at[tuple(place)].set(top_value)


def shard_levels(own_key, dims, shards, least, high):
    gain = 1.0
    for dim, parts in shards:
        draws = jax.random.uniform(jax.random.fold_in(jax.random.fold_in(own_key, 6), dim), (parts,), jnp.float32, least / len(shards), high / len(shards))
        gain = gain * jnp.repeat(jnp.exp(draws), dims[dim] // parts).reshape((-1,) + (1,) * (len(dims) - 1 - dim))
    return gain


def gaussian(stream_key, shape, spread, reach, shards=(), held_as=jnp.bfloat16):
    array = spread * jax.random.normal(stream_key, shape, jnp.float32)
    if shards:
        array = array * shard_levels(stream_key, shape, shards, -0.22, 0.18)
    return jnp.clip(array, -reach, reach).astype(held_as)


def setup_inputs(seed: int = 0) -> dict:
    key_of = jax.random.split(jax.random.key(seed), 7)
    return {
        "queries": draw_queries(jax.random.fold_in(key_of[6], 71), 0),
        "keys": draw_keys(jax.random.fold_in(key_of[6], 71), 0),
        "values": gaussian(key_of[2], (SEQ, KVH * DH), 1.0, 6.0, ((0, 8), (1, 4))),
        "block_masks": touch_ends(jax.random.randint(key_of[3], (QH, NB), 0, 2 ** LEVELS), jax.random.fold_in(key_of[3], 1), 0, (2 ** LEVELS) - 1).astype(jnp.int32),
        "residual": gaussian(key_of[4], (SEQ, D), 0.1, 1.5, ((0, 32),)),
        "norm_gain": jnp.clip(1.0 + 0.18 * jax.random.normal(key_of[5], (D,), jnp.float32), 0.099609375, 1.8984375).astype(jnp.bfloat16),
    }


MASKED_SCORE = -1e+30
EPSILON = 1e-05

def split_upper(source, axis_at, stride):
    extent = source.shape
    length = extent[axis_at]
    folded = source.reshape(extent[:axis_at] + (length // (2 * stride), 2, stride) + extent[axis_at + 1:])
    low_part = lax.index_in_dim(folded, 0, axis_at + 1, keepdims=False)
    high_part = lax.index_in_dim(folded, 1, axis_at + 1, keepdims=False)
    flattened = extent[:axis_at] + (length // 2,) + extent[axis_at + 1:]
    return (low_part.reshape(flattened), high_part.reshape(flattened))

def join_halves(low_part, high_part, axis_at, stride):
    extent = low_part.shape
    length = extent[axis_at]
    folded = extent[:axis_at] + (length // stride, 1, stride) + extent[axis_at + 1:]
    stacked = jnp.concatenate([low_part.reshape(folded), high_part.reshape(folded)], axis=axis_at + 1)
    return stacked.reshape(extent[:axis_at] + (length * 2,) + extent[axis_at + 1:])

def round_weights(weights):
    rounded = lax.optimization_barrier(weights.astype(jnp.bfloat16))
    return rounded.astype(jnp.float32)

def reference(queries, keys, values, block_masks, residual, norm_gain):
    sequence = queries.shape[0]
    block_count = sequence // BLOCK
    levels = block_count.bit_length() - 1
    group_size = QH // KVH
    scaling = DH ** (-0.5)
    query_heads = queries.reshape(block_count, BLOCK, QH, DH).transpose(2, 0, 1, 3)
    key_heads = keys.reshape(block_count, BLOCK, KVH, DH).transpose(2, 0, 1, 3)
    value_heads = values.reshape(block_count, BLOCK, KVH, DH).transpose(2, 0, 1, 3)
    causal = lax.broadcasted_iota(jnp.int32, (BLOCK, BLOCK), 0) >= lax.broadcasted_iota(jnp.int32, (BLOCK, BLOCK), 1)

    def one_head(head_number):
        kv_head = head_number // group_size
        query_part = lax.dynamic_index_in_dim(query_heads, head_number, 0, keepdims=False).astype(jnp.float32)
        key_part = lax.dynamic_index_in_dim(key_heads, kv_head, 0, keepdims=False).astype(jnp.float32)
        value_part = lax.dynamic_index_in_dim(value_heads, kv_head, 0, keepdims=False).astype(jnp.float32)
        head_bits = lax.dynamic_index_in_dim(block_masks, head_number, 0, keepdims=False)
        diagonal = jnp.einsum('nqd,nkd->nqk', query_part, key_part) * scaling
        diagonal = jnp.where(causal[None], diagonal, MASKED_SCORE)
        row_max = diagonal.max(-1)
        level_terms = []
        for bit_level in range(levels):
            stride = 2 ** bit_level
            _, query_high = split_upper(query_part, 0, stride)
            key_low, _ = split_upper(key_part, 0, stride)
            value_low, _ = split_upper(value_part, 0, stride)
            _, bits_high = split_upper(head_bits, 0, stride)
            allowed = jnp.right_shift(bits_high, bit_level) & 1 == 1
            scores = jnp.einsum('nqd,nkd->nqk', query_high, key_low) * scaling
            scores = jnp.where(allowed[:, None, None], scores, MASKED_SCORE)
            upper_max = scores.max(-1)
            row_max = jnp.maximum(row_max, join_halves(jnp.full_like(upper_max, MASKED_SCORE), upper_max, 0, stride))
            level_terms.append((bit_level, scores, value_low))
        weights = jnp.exp(diagonal - row_max[..., None])
        row_sum = weights.sum(-1)
        result = jnp.einsum('nqk,nkd->nqd', round_weights(weights), value_part)
        for bit_level, scores, value_low in level_terms:
            stride = 2 ** bit_level
            _, max_high = split_upper(row_max, 0, stride)
            weights = jnp.exp(scores - max_high[..., None])
            sum_high = weights.sum(-1)
            result_high = jnp.einsum('nqk,nkd->nqd', round_weights(weights), value_low)
            row_sum = row_sum + join_halves(jnp.zeros_like(sum_high), sum_high, 0, stride)
            result = result + join_halves(jnp.zeros_like(result_high), result_high, 0, stride)
        return (result / row_sum[..., None]).astype(jnp.bfloat16)
    attended = lax.map(one_head, jnp.arange(QH, dtype=jnp.int32))
    attended = attended.transpose(1, 2, 0, 3).reshape(sequence, QH * DH)
    summed = residual.astype(jnp.float32) + attended.astype(jnp.float32)
    stream = summed.astype(jnp.bfloat16)
    normed = summed * lax.rsqrt(lax.optimization_barrier(jnp.mean(summed * summed, axis=-1, keepdims=True)) + EPSILON) * norm_gain.astype(jnp.float32)
    return (stream, normed.astype(jnp.bfloat16))
```

```python
import functools

import jax
import jax.numpy as jnp
from jax import lax
from jax.experimental import pallas as pl
from jax.experimental.pallas import tpu as pltpu
from jax.sharding import PartitionSpec as P

DH = 128
BLOCK = 128
MASKED_SCORE = -1e30
EPSILON = 1e-05
LOG2_E = 1.4426950408889634
MESH = pl.DeviceIdType.MESH


def rows_of(block):
    return pl.ds(pl.multiple_of(block * BLOCK, BLOCK), BLOCK)


def attention_kernel(
    sizes,
    masks,
    q_hbm,
    k_hbm,
    v_hbm,
    out,
    q_own,
    k_all,
    v_all,
    ready,
    load_sem,
    kv_send,
    kv_recv,
    att_send,
    att_recv,
    own_sem,
):
    ctx_bits, nh, groups, per_group, blocks, per_owner = sizes
    local_bits = blocks.bit_length() - 1
    width = groups * per_group * DH
    others = (nh - 1) * per_owner
    c = lax.axis_index("ctx")
    h = lax.axis_index("head")
    bit_of = [(c // 2**b) % 2 for b in range(ctx_bits)]

    loads = [
        pltpu.make_async_copy(k_hbm, k_all.at[0], load_sem.at[0]),
        pltpu.make_async_copy(v_hbm, v_all.at[0], load_sem.at[1]),
        pltpu.make_async_copy(q_hbm, q_own, load_sem.at[2]),
    ]
    for load in loads:
        load.start()

    barrier = pltpu.get_barrier_semaphore()
    for b in range(ctx_bits):
        partner = c + 2**b - 2 * 2**b * bit_of[b]
        pl.semaphore_signal(barrier, inc=1, device_id=(partner, h), device_id_type=MESH)
    for d in range(1, nh):
        pl.semaphore_signal(barrier, inc=1, device_id=(c, (h + d) % nh), device_id_type=MESH)
    pl.semaphore_wait(barrier, ctx_bits + nh - 1)

    def block_at(step):
        owner = (h + 1 + step // per_owner) % nh
        return owner, step % per_owner, owner * per_owner + step % per_owner

    def kv_copies(b, block, target):
        return [
            pltpu.make_async_remote_copy(
                src_ref=source.at[rows_of(block)],
                dst_ref=landing.at[1 + b, rows_of(block)],
                send_sem=kv_send.at[n, b, block],
                recv_sem=kv_recv.at[n, b, block],
                device_id=(target, h),
                device_id_type=MESH,
            )
            for n, (source, landing) in enumerate(((k_hbm, k_all), (v_hbm, v_all)))
        ]

    def send_step(step, carry):
        _, _, block = block_at(step)
        for b in reversed(range(ctx_bits)):

            @pl.when(bit_of[b] == 0)
            def _():
                for copy in kv_copies(b, block, c + 2**b):
                    copy.start()

        return carry

    lax.fori_loop(0, blocks, send_step, 0)
    for load in loads:
        load.wait()

    causal = lax.broadcasted_iota(jnp.int32, (BLOCK, BLOCK), 0) >= lax.broadcasted_iota(
        jnp.int32, (BLOCK, BLOCK), 1
    )

    def attend(block, step):
        for b in range(ctx_bits):

            @pl.when(bit_of[b] == 1)
            def _():
                for copy in kv_copies(b, block, c - 2**b):
                    copy.wait_recv()

        here = [(block // 2**b) % 2 for b in range(local_bits)]
        places = [(0, block)]
        places += [(0, block - here[b] * 2**b) for b in range(local_bits)]
        places += [(bit_of[b] * (1 + b), block) for b in range(ctx_bits)]
        usable = here + bit_of
        for g in range(groups):
            columns = pl.ds(g * DH, DH)
            keys = jnp.concatenate([k_all[s, rows_of(j), columns] for s, j in places], axis=0)
            values = jnp.concatenate([v_all[s, rows_of(j), columns] for s, j in places], axis=0)
            queries = jnp.concatenate(
                [
                    q_own[rows_of(block), pl.ds((g * per_group + j) * DH, DH)]
                    for j in range(per_group)
                ],
                axis=0,
            )
            scores = lax.dot_general(
                queries, keys, (((1,), (1,)), ((), ())), preferred_element_type=jnp.float32
            )
            weights, sums = [], []
            for j in range(per_group):
                bits = masks[g * per_group + j, block]
                part = scores[j * BLOCK : (j + 1) * BLOCK]
                pieces = [jnp.where(causal, part[:, :BLOCK], MASKED_SCORE)]
                for n, flag in enumerate(usable):
                    allowed = ((bits >> n) & 1) * flag
                    bias = (1 - allowed).astype(jnp.float32) * MASKED_SCORE
                    pieces.append(part[:, (n + 1) * BLOCK : (n + 2) * BLOCK] + bias)
                top = functools.reduce(jnp.maximum, pieces)
                top = jnp.max(top, axis=-1, keepdims=True)
                raised = [jnp.exp2((piece - top) * (DH**-0.5 * LOG2_E)) for piece in pieces]
                sums.append(jnp.sum(functools.reduce(jnp.add, raised), axis=-1, keepdims=True))
                weights.append(
                    jnp.concatenate([piece.astype(jnp.bfloat16) for piece in raised], axis=1)
                )
            weighted = jnp.dot(
                jnp.concatenate(weights, axis=0), values, preferred_element_type=jnp.float32
            )
            for j in range(per_group):
                ready[step, :, pl.ds((g * per_group + j) * DH, DH)] = (
                    weighted[j * BLOCK : (j + 1) * BLOCK] / sums[j]
                ).astype(jnp.bfloat16)

    def att_copy(step, owner, source_head, place):
        return pltpu.make_async_remote_copy(
            src_ref=ready.at[step],
            dst_ref=out.at[rows_of(place), pl.ds(pl.multiple_of(source_head * width, width), width)],
            send_sem=att_send.at[step],
            recv_sem=att_recv.at[source_head, place],
            device_id=(c, owner),
            device_id_type=MESH,
        )

    def own_copy(step):
        return pltpu.make_async_copy(
            ready.at[step],
            out.at[rows_of(step - others), pl.ds(pl.multiple_of(h * width, width), width)],
            own_sem.at[step - others],
        )

    def compute_step(step, carry):
        owner, place, block = block_at(step)
        attend(block, step)

        @pl.when(step < others)
        def _():
            att_copy(step, owner, h, place).start()

        @pl.when(step >= others)
        def _():
            own_copy(step).start()

        return carry

    lax.fori_loop(0, blocks, compute_step, 0)

    for place in range(per_owner):
        own_copy(others + place).wait()
        for d in range(1, nh):
            source_head = (h + d) % nh
            att_copy(0, source_head, source_head, place).wait_recv()

    def drain(step, carry):
        owner, place, block = block_at(step)
        for b in range(ctx_bits):

            @pl.when(bit_of[b] == 0)
            def _():
                for copy in kv_copies(b, block, c + 2**b):
                    copy.wait_send()

        @pl.when(step < others)
        def _():
            att_copy(step, owner, h, place).wait_send()

        return carry

    lax.fori_loop(0, blocks, drain, 0)


def norm_kernel(residual, attended, gain, stream, normed):
    summed = residual[...].astype(jnp.float32) + attended[...].astype(jnp.float32)
    stream[...] = summed.astype(jnp.bfloat16)
    mean = jnp.mean(summed * summed, axis=-1, keepdims=True)
    normed[...] = (
        summed * lax.rsqrt(mean + EPSILON) * gain[...].astype(jnp.float32)
    ).astype(jnp.bfloat16)


def shards(queries, keys, values, block_masks, residual, norm_gain):
    tokens, width = queries.shape
    kv_width = keys.shape[1]
    blocks = tokens // BLOCK
    groups = kv_width // DH
    per_group = width // kv_width
    nh = lax.axis_size("head")
    ctx_bits = lax.axis_size("ctx").bit_length() - 1
    rows, full = residual.shape
    per_owner = rows // BLOCK
    sizes = (ctx_bits, nh, groups, per_group, blocks, per_owner)
    in_any = pl.BlockSpec(memory_space=pl.ANY)
    attended = pl.pallas_call(
        functools.partial(attention_kernel, sizes),
        out_shape=jax.ShapeDtypeStruct((rows, full), jnp.bfloat16),
        in_specs=[pl.BlockSpec(memory_space=pltpu.SMEM), in_any, in_any, in_any],
        out_specs=in_any,
        scratch_shapes=[
            pltpu.VMEM((tokens, width), jnp.bfloat16),
            pltpu.VMEM((1 + ctx_bits, tokens, kv_width), jnp.bfloat16),
            pltpu.VMEM((1 + ctx_bits, tokens, kv_width), jnp.bfloat16),
            pltpu.VMEM((blocks, BLOCK, width), jnp.bfloat16),
            pltpu.SemaphoreType.DMA((3,)),
            pltpu.SemaphoreType.DMA((2, ctx_bits, blocks)),
            pltpu.SemaphoreType.DMA((2, ctx_bits, blocks)),
            pltpu.SemaphoreType.DMA((blocks,)),
            pltpu.SemaphoreType.DMA((nh, per_owner)),
            pltpu.SemaphoreType.DMA((per_owner,)),
        ],
        compiler_params=pltpu.CompilerParams(
            collective_id=0, has_side_effects=True, vmem_limit_bytes=48 * 2**20
        ),
        name="attention",
    )(block_masks, queries, keys, values)
    tile = min(rows, 64)
    by_rows = pl.BlockSpec((tile, full), lambda n: (n, 0))
    return pl.pallas_call(
        norm_kernel,
        grid=(rows // tile,),
        out_shape=(jax.ShapeDtypeStruct((rows, full), jnp.bfloat16),) * 2,
        in_specs=[by_rows, by_rows, pl.BlockSpec((1, full), lambda n: (0, 0))],
        out_specs=(by_rows, by_rows),
        compiler_params=pltpu.CompilerParams(vmem_limit_bytes=32 * 2**20),
        name="add_norm",
    )(residual, attended, norm_gain.reshape(1, full))


def solution(mesh):
    in_specs = (
        P("ctx", "head"),
        P("ctx", "head"),
        P("ctx", "head"),
        P("head", "ctx"),
        P(("ctx", "head"), None),
        P(),
    )
    out_specs = (P(("ctx", "head"), None), P(("ctx", "head"), None))
    return jax.shard_map(shards, mesh=mesh, in_specs=in_specs, out_specs=out_specs, check_vma=False)
```

```python
import functools

import jax
import jax.numpy as jnp
from jax import lax
from jax.experimental import pallas as pl
from jax.experimental.pallas import tpu as pltpu
from jax.sharding import PartitionSpec as P

DH = 128
BLOCK = 128
MASKED_SCORE = -1e30
EPSILON = 1e-05
LOG2_E = 1.4426950408889634
MESH = pl.DeviceIdType.MESH


def rows_of(block):
    return pl.ds(pl.multiple_of(block * BLOCK, BLOCK), BLOCK)


def attention_kernel(
    sizes,
    masks_hbm,
    q_hbm,
    k_hbm,
    v_hbm,
    out,
    masks,
    q_own,
    k_all,
    v_all,
    ready,
    load_sem,
    kv_send,
    kv_recv,
    att_send,
    att_recv,
    own_sem,
):
    ctx_bits, nh, groups, per_group, blocks, per_owner = sizes
    local_bits = blocks.bit_length() - 1
    width = groups * per_group * DH
    others = (nh - 1) * per_owner
    c = lax.axis_index("ctx")
    h = lax.axis_index("head")
    bit_of = [(c // 2**b) % 2 for b in range(ctx_bits)]

    loads = [
        pltpu.make_async_copy(k_hbm, k_all.at[0], load_sem.at[0]),
        pltpu.make_async_copy(v_hbm, v_all.at[0], load_sem.at[1]),
        pltpu.make_async_copy(q_hbm, q_own, load_sem.at[2]),
        pltpu.make_async_copy(masks_hbm, masks, load_sem.at[3]),
    ]
    for load in loads:
        load.start()

    barrier = pltpu.get_barrier_semaphore()
    for b in range(ctx_bits):
        partner = c + 2**b - 2 * 2**b * bit_of[b]
        pl.semaphore_signal(barrier, inc=1, device_id=(partner, h), device_id_type=MESH)
    for d in range(1, nh):
        pl.semaphore_signal(barrier, inc=1, device_id=(c, (h + d) % nh), device_id_type=MESH)
    pl.semaphore_wait(barrier, ctx_bits + nh - 1)

    def block_at(step):
        owner = (h + 1 + step // per_owner) % nh
        return owner, step % per_owner, owner * per_owner + step % per_owner

    def kv_copies(b, block, target):
        return [
            pltpu.make_async_remote_copy(
                src_ref=source.at[rows_of(block)],
                dst_ref=landing.at[1 + b, rows_of(block)],
                send_sem=kv_send.at[n, b, block],
                recv_sem=kv_recv.at[n, b, block],
                device_id=(target, h),
                device_id_type=MESH,
            )
            for n, (source, landing) in enumerate(((k_hbm, k_all), (v_hbm, v_all)))
        ]

    def send_step(step, carry):
        _, _, block = block_at(step)
        for b in reversed(range(ctx_bits)):

            @pl.when(bit_of[b] == 0)
            def _():
                for copy in kv_copies(b, block, c + 2**b):
                    copy.start()

        return carry

    lax.fori_loop(0, blocks, send_step, 0)
    for load in loads:
        load.wait()

    causal = lax.broadcasted_iota(jnp.int32, (BLOCK, BLOCK), 0) >= lax.broadcasted_iota(
        jnp.int32, (BLOCK, BLOCK), 1
    )

    def attend(block, step):
        for b in range(ctx_bits):

            @pl.when(bit_of[b] == 1)
            def _():
                for copy in kv_copies(b, block, c - 2**b):
                    copy.wait_recv()

        here = [(block // 2**b) % 2 for b in range(local_bits)]
        places = [(0, block)]
        places += [(0, block - here[b] * 2**b) for b in range(local_bits)]
        places += [(bit_of[b] * (1 + b), block) for b in range(ctx_bits)]
        usable = here + bit_of
        for g in range(groups):
            columns = pl.ds(g * DH, DH)
            keys = jnp.concatenate([k_all[s, rows_of(j), columns] for s, j in places], axis=0)
            values = jnp.concatenate([v_all[s, rows_of(j), columns] for s, j in places], axis=0)
            queries = jnp.concatenate(
                [
                    q_own[rows_of(block), pl.ds((g * per_group + j) * DH, DH)]
                    for j in range(per_group)
                ],
                axis=0,
            )
            scores = lax.dot_general(
                queries, keys, (((1,), (1,)), ((), ())), preferred_element_type=jnp.float32
            )
            weights, sums = [], []
            for j in range(per_group):
                bits = masks[g * per_group + j, block]
                part = scores[j * BLOCK : (j + 1) * BLOCK]
                pieces = [jnp.where(causal, part[:, :BLOCK], MASKED_SCORE)]
                for n, flag in enumerate(usable):
                    allowed = ((bits >> n) & 1) * flag
                    bias = (1 - allowed).astype(jnp.float32) * MASKED_SCORE
                    pieces.append(part[:, (n + 1) * BLOCK : (n + 2) * BLOCK] + bias)
                top = functools.reduce(jnp.maximum, pieces)
                top = jnp.max(top, axis=-1, keepdims=True)
                raised = [jnp.exp2((piece - top) * (DH**-0.5 * LOG2_E)) for piece in pieces]
                sums.append(jnp.sum(functools.reduce(jnp.add, raised), axis=-1, keepdims=True))
                weights.append(
                    jnp.concatenate([piece.astype(jnp.bfloat16) for piece in raised], axis=1)
                )
            weighted = jnp.dot(
                jnp.concatenate(weights, axis=0), values, preferred_element_type=jnp.float32
            )
            for j in range(per_group):
                ready[step, :, pl.ds((g * per_group + j) * DH, DH)] = (
                    weighted[j * BLOCK : (j + 1) * BLOCK] / sums[j]
                ).astype(jnp.bfloat16)

    def att_copy(step, owner, source_head, place):
        return pltpu.make_async_remote_copy(
            src_ref=ready.at[step],
            dst_ref=out.at[rows_of(place), pl.ds(pl.multiple_of(source_head * width, width), width)],
            send_sem=att_send.at[step],
            recv_sem=att_recv.at[source_head, place],
            device_id=(c, owner),
            device_id_type=MESH,
        )

    def own_copy(step):
        return pltpu.make_async_copy(
            ready.at[step],
            out.at[rows_of(step - others), pl.ds(pl.multiple_of(h * width, width), width)],
            own_sem.at[step - others],
        )

    def compute_step(step, carry):
        owner, place, block = block_at(step)
        attend(block, step)

        @pl.when(step < others)
        def _():
            att_copy(step, owner, h, place).start()

        @pl.when(step >= others)
        def _():
            own_copy(step).start()

        return carry

    lax.fori_loop(0, blocks, compute_step, 0)

    for place in range(per_owner):
        own_copy(others + place).wait()
        for d in range(1, nh):
            source_head = (h + d) % nh
            att_copy(0, source_head, source_head, place).wait_recv()

    def drain(step, carry):
        owner, place, block = block_at(step)
        for b in range(ctx_bits):

            @pl.when(bit_of[b] == 0)
            def _():
                for copy in kv_copies(b, block, c + 2**b):
                    copy.wait_send()

        @pl.when(step < others)
        def _():
            att_copy(step, owner, h, place).wait_send()

        return carry

    lax.fori_loop(0, blocks, drain, 0)


def norm_kernel(residual, attended, gain, stream, normed):
    summed = residual[...].astype(jnp.float32) + attended[...].astype(jnp.float32)
    stream[...] = summed.astype(jnp.bfloat16)
    mean = jnp.mean(summed * summed, axis=-1, keepdims=True)
    normed[...] = (
        summed * lax.rsqrt(mean + EPSILON) * gain[...].astype(jnp.float32)[None, :]
    ).astype(jnp.bfloat16)


def shards(queries, keys, values, block_masks, residual, norm_gain):
    tokens, width = queries.shape
    kv_width = keys.shape[1]
    blocks = tokens // BLOCK
    groups = kv_width // DH
    per_group = width // kv_width
    nh = lax.axis_size("head")
    ctx_bits = lax.axis_size("ctx").bit_length() - 1
    rows, full = residual.shape
    per_owner = rows // BLOCK
    sizes = (ctx_bits, nh, groups, per_group, blocks, per_owner)
    in_hbm = pl.BlockSpec(memory_space=pltpu.HBM)
    attended = pl.pallas_call(
        functools.partial(attention_kernel, sizes),
        out_shape=jax.ShapeDtypeStruct((rows, full), jnp.bfloat16),
        in_specs=[in_hbm] * 4,
        out_specs=in_hbm,
        scratch_shapes=[
            pltpu.SMEM(block_masks.shape, jnp.int32),
            pltpu.VMEM((tokens, width), jnp.bfloat16),
            pltpu.VMEM((1 + ctx_bits, tokens, kv_width), jnp.bfloat16),
            pltpu.VMEM((1 + ctx_bits, tokens, kv_width), jnp.bfloat16),
            pltpu.VMEM((blocks, BLOCK, width), jnp.bfloat16),
            pltpu.SemaphoreType.DMA((4,)),
            pltpu.SemaphoreType.DMA((2, ctx_bits, blocks)),
            pltpu.SemaphoreType.DMA((2, ctx_bits, blocks)),
            pltpu.SemaphoreType.DMA((blocks,)),
            pltpu.SemaphoreType.DMA((nh, per_owner)),
            pltpu.SemaphoreType.DMA((per_owner,)),
        ],
        compiler_params=pltpu.CompilerParams(
            collective_id=0, has_side_effects=True, vmem_limit_bytes=48 * 2**20
        ),
        name="attention",
    )(*(pltpu.with_memory_space_constraint(x, pltpu.HBM) for x in (block_masks, queries, keys, values)))
    tile = min(rows, 64)
    by_rows = pl.BlockSpec((tile, full), lambda n: (n, 0))
    return pl.pallas_call(
        norm_kernel,
        grid=(rows // tile,),
        out_shape=(jax.ShapeDtypeStruct((rows, full), jnp.bfloat16),) * 2,
        in_specs=[by_rows, by_rows, pl.BlockSpec((full,), lambda n: (0,))],
        out_specs=(by_rows, by_rows),
        compiler_params=pltpu.CompilerParams(vmem_limit_bytes=32 * 2**20),
        name="add_norm",
    )(residual, attended, norm_gain)


def solution(mesh):
    in_specs = (
        P("ctx", "head"),
        P("ctx", "head"),
        P("ctx", "head"),
        P("head", "ctx"),
        P(("ctx", "head"), None),
        P(),
    )
    out_specs = (P(("ctx", "head"), None), P(("ctx", "head"), None))
    return jax.shard_map(shards, mesh=mesh, in_specs=in_specs, out_specs=out_specs, check_vma=False)
```

```python
import functools

import jax
import jax.numpy as jnp
from jax import lax
from jax.experimental import pallas as pl
from jax.experimental.pallas import tpu as pltpu
from jax.sharding import PartitionSpec as P

DH = 128
BLOCK = 128
MASKED_SCORE = -1e30
EPSILON = 1e-05
LOG2_E = 1.4426950408889634
MESH = pl.DeviceIdType.MESH


def rows_of(block):
    return pl.ds(pl.multiple_of(block * BLOCK, BLOCK), BLOCK)


def attention_kernel(
    sizes,
    masks_hbm,
    q_hbm,
    k_hbm,
    v_hbm,
    out,
    masks,
    q_own,
    k_all,
    v_all,
    ready,
    load_sem,
    kv_send,
    kv_recv,
    att_send,
    att_recv,
    own_sem,
):
    ctx_bits, nh, groups, per_group, blocks, per_owner = sizes
    local_bits = blocks.bit_length() - 1
    width = groups * per_group * DH
    others = (nh - 1) * per_owner
    c = lax.axis_index("ctx")
    h = lax.axis_index("head")
    bit_of = [(c // 2**b) % 2 for b in range(ctx_bits)]

    loads = [
        pltpu.make_async_copy(k_hbm, k_all.at[0], load_sem.at[0]),
        pltpu.make_async_copy(v_hbm, v_all.at[0], load_sem.at[1]),
        pltpu.make_async_copy(q_hbm, q_own, load_sem.at[2]),
        pltpu.make_async_copy(masks_hbm, masks, load_sem.at[3]),
    ]
    for load in loads:
        load.start()

    barrier = pltpu.get_barrier_semaphore()
    for b in range(ctx_bits):
        partner = c + 2**b - 2 * 2**b * bit_of[b]
        pl.semaphore_signal(barrier, inc=1, device_id=(partner, h), device_id_type=MESH)
    for d in range(1, nh):
        pl.semaphore_signal(barrier, inc=1, device_id=(c, (h + d) % nh), device_id_type=MESH)
    pl.semaphore_wait(barrier, ctx_bits + nh - 1)

    def block_at(step):
        owner = (h + 1 + step // per_owner) % nh
        return owner, step % per_owner, owner * per_owner + step % per_owner

    def kv_copies(b, block, target):
        return [
            pltpu.make_async_remote_copy(
                src_ref=source.at[rows_of(block)],
                dst_ref=landing.at[1 + b, rows_of(block)],
                send_sem=kv_send.at[n, b, block],
                recv_sem=kv_recv.at[n, b, block],
                device_id=(target, h),
                device_id_type=MESH,
            )
            for n, (source, landing) in enumerate(((k_hbm, k_all), (v_hbm, v_all)))
        ]

    def send_step(step, carry):
        _, _, block = block_at(step)
        for b in reversed(range(ctx_bits)):

            @pl.when(bit_of[b] == 0)
            def _():
                for copy in kv_copies(b, block, c + 2**b):
                    copy.start()

        return carry

    lax.fori_loop(0, blocks, send_step, 0)
    for load in loads:
        load.wait()

    causal = lax.broadcasted_iota(jnp.int32, (BLOCK, BLOCK), 0) >= lax.broadcasted_iota(
        jnp.int32, (BLOCK, BLOCK), 1
    )

    def sources(places, column):
        columns = pl.ds(column * DH, DH)
        return tuple(
            jnp.concatenate([held[s, rows_of(j), columns] for s, j in places], axis=0)
            for held in (k_all, v_all)
        )

    def scored(g, block, keys):
        queries = jnp.concatenate(
            [q_own[rows_of(block), pl.ds((g * per_group + j) * DH, DH)] for j in range(per_group)],
            axis=0,
        )
        return lax.dot_general(
            queries, keys, (((1,), (1,)), ((), ())), preferred_element_type=jnp.float32
        )

    def biased(piece, bits, level, flag):
        allowed = ((bits >> level) & 1) * flag
        return piece + (1 - allowed).astype(jnp.float32) * MASKED_SCORE

    def raised(pieces, top):
        weights = [jnp.exp2((piece - top) * (DH**-0.5 * LOG2_E)) for piece in pieces]
        total = jnp.sum(functools.reduce(jnp.add, weights), axis=-1, keepdims=True)
        return jnp.concatenate([w.astype(jnp.bfloat16) for w in weights], axis=1), total

    def row_top(pieces):
        return jnp.max(functools.reduce(jnp.maximum, pieces), axis=-1, keepdims=True)

    def cut(scores, j, count):
        part = scores[j * BLOCK : (j + 1) * BLOCK]
        return [part[:, n * BLOCK : (n + 1) * BLOCK] for n in range(count)]

    def attend(block, step):
        here = [(block // 2**b) % 2 for b in range(local_bits)]
        near = [(0, block)] + [(0, block - here[b] * 2**b) for b in range(local_bits)]
        far = [(bit_of[b] * (1 + b), block) for b in range(ctx_bits)]
        partial = []
        for g in range(groups):
            keys, values = sources(near, g)
            scores = scored(g, block, keys)
            weights, tops, sums = [], [], []
            for j in range(per_group):
                bits = masks[g * per_group + j, block]
                pieces = cut(scores, j, 1 + local_bits)
                pieces = [jnp.where(causal, pieces[0], MASKED_SCORE)] + [
                    biased(piece, bits, b, here[b]) for b, piece in enumerate(pieces[1:])
                ]
                tops.append(row_top(pieces))
                weight, total = raised(pieces, tops[-1])
                weights.append(weight)
                sums.append(total)
            weighted = jnp.dot(
                jnp.concatenate(weights, axis=0), values, preferred_element_type=jnp.float32
            )
            partial.append((tops, sums, weighted))

        for b in range(ctx_bits):

            @pl.when(bit_of[b] == 1)
            def _():
                for copy in kv_copies(b, block, c - 2**b):
                    copy.wait_recv()

        for g in range(groups):
            tops, sums, weighted = partial[g]
            keys, values = sources(far, g)
            scores = scored(g, block, keys)
            weights, factors, totals = [], [], []
            for j in range(per_group):
                bits = masks[g * per_group + j, block]
                pieces = [
                    biased(piece, bits, local_bits + b, bit_of[b])
                    for b, piece in enumerate(cut(scores, j, ctx_bits))
                ]
                top = jnp.maximum(tops[j], row_top(pieces))
                weight, total = raised(pieces, top)
                factor = jnp.exp2((tops[j] - top) * (DH**-0.5 * LOG2_E))
                weights.append(weight)
                factors.append(factor)
                totals.append(sums[j] * factor + total)
            added = jnp.dot(
                jnp.concatenate(weights, axis=0), values, preferred_element_type=jnp.float32
            )
            for j in range(per_group):
                lines = slice(j * BLOCK, (j + 1) * BLOCK)
                ready[step, :, pl.ds((g * per_group + j) * DH, DH)] = (
                    (weighted[lines] * factors[j] + added[lines]) / totals[j]
                ).astype(jnp.bfloat16)

    def att_copy(step, owner, source_head, place):
        return pltpu.make_async_remote_copy(
            src_ref=ready.at[step],
            dst_ref=out.at[rows_of(place), pl.ds(pl.multiple_of(source_head * width, width), width)],
            send_sem=att_send.at[step],
            recv_sem=att_recv.at[source_head, place],
            device_id=(c, owner),
            device_id_type=MESH,
        )

    def own_copy(step):
        return pltpu.make_async_copy(
            ready.at[step],
            out.at[rows_of(step - others), pl.ds(pl.multiple_of(h * width, width), width)],
            own_sem.at[step - others],
        )

    def compute_step(step, carry):
        owner, place, block = block_at(step)
        attend(block, step)

        @pl.when(step < others)
        def _():
            att_copy(step, owner, h, place).start()

        @pl.when(step >= others)
        def _():
            own_copy(step).start()

        return carry

    lax.fori_loop(0, blocks, compute_step, 0)

    for place in range(per_owner):
        own_copy(others + place).wait()
        for d in range(1, nh):
            source_head = (h + d) % nh
            att_copy(0, source_head, source_head, place).wait_recv()

    def drain(step, carry):
        owner, place, block = block_at(step)
        for b in range(ctx_bits):

            @pl.when(bit_of[b] == 0)
            def _():
                for copy in kv_copies(b, block, c + 2**b):
                    copy.wait_send()

        @pl.when(step < others)
        def _():
            att_copy(step, owner, h, place).wait_send()

        return carry

    lax.fori_loop(0, blocks, drain, 0)


def norm_kernel(residual, attended, gain, stream, normed):
    summed = residual[...].astype(jnp.float32) + attended[...].astype(jnp.float32)
    stream[...] = summed.astype(jnp.bfloat16)
    mean = jnp.mean(summed * summed, axis=-1, keepdims=True)
    normed[...] = (
        summed * lax.rsqrt(mean + EPSILON) * gain[...].astype(jnp.float32)[None, :]
    ).astype(jnp.bfloat16)


def shards(queries, keys, values, block_masks, residual, norm_gain):
    tokens, width = queries.shape
    kv_width = keys.shape[1]
    blocks = tokens // BLOCK
    groups = kv_width // DH
    per_group = width // kv_width
    nh = lax.axis_size("head")
    ctx_bits = lax.axis_size("ctx").bit_length() - 1
    rows, full = residual.shape
    per_owner = rows // BLOCK
    sizes = (ctx_bits, nh, groups, per_group, blocks, per_owner)
    in_hbm = pl.BlockSpec(memory_space=pltpu.HBM)
    attended = pl.pallas_call(
        functools.partial(attention_kernel, sizes),
        out_shape=jax.ShapeDtypeStruct((rows, full), jnp.bfloat16),
        in_specs=[in_hbm] * 4,
        out_specs=in_hbm,
        scratch_shapes=[
            pltpu.SMEM(block_masks.shape, jnp.int32),
            pltpu.VMEM((tokens, width), jnp.bfloat16),
            pltpu.VMEM((1 + ctx_bits, tokens, kv_width), jnp.bfloat16),
            pltpu.VMEM((1 + ctx_bits, tokens, kv_width), jnp.bfloat16),
            pltpu.VMEM((blocks, BLOCK, width), jnp.bfloat16),
            pltpu.SemaphoreType.DMA((4,)),
            pltpu.SemaphoreType.DMA((2, ctx_bits, blocks)),
            pltpu.SemaphoreType.DMA((2, ctx_bits, blocks)),
            pltpu.SemaphoreType.DMA((blocks,)),
            pltpu.SemaphoreType.DMA((nh, per_owner)),
            pltpu.SemaphoreType.DMA((per_owner,)),
        ],
        compiler_params=pltpu.CompilerParams(
            collective_id=0, has_side_effects=True, vmem_limit_bytes=48 * 2**20
        ),
        name="attention",
    )(*(pltpu.with_memory_space_constraint(x, pltpu.HBM) for x in (block_masks, queries, keys, values)))
    tile = min(rows, 128)
    by_rows = pl.BlockSpec((tile, full), lambda n: (n, 0))
    return pl.pallas_call(
        norm_kernel,
        grid=(rows // tile,),
        out_shape=(jax.ShapeDtypeStruct((rows, full), jnp.bfloat16),) * 2,
        in_specs=[by_rows, by_rows, pl.BlockSpec((full,), lambda n: (0,))],
        out_specs=(by_rows, by_rows),
        compiler_params=pltpu.CompilerParams(vmem_limit_bytes=32 * 2**20),
        name="add_norm",
    )(residual, attended, norm_gain)


def solution(mesh):
    in_specs = (
        P("ctx", "head"),
        P("ctx", "head"),
        P("ctx", "head"),
        P("head", "ctx"),
        P(("ctx", "head"), None),
        P(),
    )
    out_specs = (P(("ctx", "head"), None), P(("ctx", "head"), None))
    return jax.shard_map(shards, mesh=mesh, in_specs=in_specs, out_specs=out_specs, check_vma=False)
```

```python
import functools

import jax
import jax.numpy as jnp
from jax import lax
from jax.experimental import pallas as pl
from jax.experimental.pallas import tpu as pltpu
from jax.sharding import PartitionSpec as P

DH = 128
BLOCK = 128
MASKED_SCORE = -1e30
EPSILON = 1e-05
LOG2_E = 1.4426950408889634
MESH = pl.DeviceIdType.MESH


def rows_of(block):
    return pl.ds(pl.multiple_of(block * BLOCK, BLOCK), BLOCK)


def attention_kernel(
    sizes,
    masks_hbm,
    q_hbm,
    k_hbm,
    v_hbm,
    out,
    masks,
    q_own,
    k_all,
    v_all,
    ready,
    load_sem,
    kv_send,
    kv_recv,
    att_send,
    att_recv,
    own_sem,
):
    ctx_bits, nh, groups, per_group, blocks, per_owner = sizes
    local_bits = blocks.bit_length() - 1
    width = groups * per_group * DH
    others = (nh - 1) * per_owner
    c = lax.axis_index("ctx")
    h = lax.axis_index("head")
    bit_of = [(c // 2**b) % 2 for b in range(ctx_bits)]

    loads = [
        pltpu.make_async_copy(k_hbm, k_all.at[0], load_sem.at[0]),
        pltpu.make_async_copy(v_hbm, v_all.at[0], load_sem.at[1]),
        pltpu.make_async_copy(q_hbm, q_own, load_sem.at[2]),
        pltpu.make_async_copy(masks_hbm, masks, load_sem.at[3]),
    ]
    for load in loads:
        load.start()

    barrier = pltpu.get_barrier_semaphore()
    for b in range(ctx_bits):
        partner = c + 2**b - 2 * 2**b * bit_of[b]
        pl.semaphore_signal(barrier, inc=1, device_id=(partner, h), device_id_type=MESH)
    for d in range(1, nh):
        pl.semaphore_signal(barrier, inc=1, device_id=(c, (h + d) % nh), device_id_type=MESH)
    pl.semaphore_wait(barrier, ctx_bits + nh - 1)

    def block_at(step):
        owner = (h + 1 + step // per_owner) % nh
        return owner, step % per_owner, owner * per_owner + step % per_owner

    def kv_copies(b, block, target):
        return [
            pltpu.make_async_remote_copy(
                src_ref=source.at[rows_of(block)],
                dst_ref=landing.at[1 + b, rows_of(block)],
                send_sem=kv_send.at[n, b, block],
                recv_sem=kv_recv.at[n, b, block],
                device_id=(target, h),
                device_id_type=MESH,
            )
            for n, (source, landing) in enumerate(((k_hbm, k_all), (v_hbm, v_all)))
        ]

    def send_step(step, carry):
        _, _, block = block_at(step)
        for n in range(2):
            for b in reversed(range(ctx_bits)):

                @pl.when(bit_of[b] == 0)
                def _():
                    kv_copies(b, block, c + 2**b)[n].start()

        return carry

    lax.fori_loop(0, blocks, send_step, 0)
    for load in loads:
        load.wait()

    causal = lax.broadcasted_iota(jnp.int32, (BLOCK, BLOCK), 0) >= lax.broadcasted_iota(
        jnp.int32, (BLOCK, BLOCK), 1
    )

    def gathered(held, places, column):
        columns = pl.ds(column * DH, DH)
        return jnp.concatenate([held[s, rows_of(j), columns] for s, j in places], axis=0)

    def scored(g, block, keys):
        queries = jnp.concatenate(
            [q_own[rows_of(block), pl.ds((g * per_group + j) * DH, DH)] for j in range(per_group)],
            axis=0,
        )
        return lax.dot_general(
            queries, keys, (((1,), (1,)), ((), ())), preferred_element_type=jnp.float32
        )

    def biased(piece, bits, level, flag):
        allowed = ((bits >> level) & 1) * flag
        return piece + (1 - allowed).astype(jnp.float32) * MASKED_SCORE

    def raised(pieces, top):
        weights = [jnp.exp2((piece - top) * (DH**-0.5 * LOG2_E)) for piece in pieces]
        total = jnp.sum(functools.reduce(jnp.add, weights), axis=-1, keepdims=True)
        return jnp.concatenate([w.astype(jnp.bfloat16) for w in weights], axis=1), total

    def row_top(pieces):
        return jnp.max(functools.reduce(jnp.maximum, pieces), axis=-1, keepdims=True)

    def cut(scores, j, count):
        part = scores[j * BLOCK : (j + 1) * BLOCK]
        return [part[:, n * BLOCK : (n + 1) * BLOCK] for n in range(count)]

    def attend(block, step):
        here = [(block // 2**b) % 2 for b in range(local_bits)]
        near = [(0, block)] + [(0, block - here[b] * 2**b) for b in range(local_bits)]
        far = [(bit_of[b] * (1 + b), block) for b in range(ctx_bits)]
        partial = []
        for g in range(groups):
            keys, values = gathered(k_all, near, g), gathered(v_all, near, g)
            scores = scored(g, block, keys)
            weights, tops, sums = [], [], []
            for j in range(per_group):
                bits = masks[g * per_group + j, block]
                pieces = cut(scores, j, 1 + local_bits)
                pieces = [jnp.where(causal, pieces[0], MASKED_SCORE)] + [
                    biased(piece, bits, b, here[b]) for b, piece in enumerate(pieces[1:])
                ]
                tops.append(row_top(pieces))
                weight, total = raised(pieces, tops[-1])
                weights.append(weight)
                sums.append(total)
            weighted = jnp.dot(
                jnp.concatenate(weights, axis=0), values, preferred_element_type=jnp.float32
            )
            partial.append((tops, sums, weighted))

        def arrived(n):
            for b in range(ctx_bits):

                @pl.when(bit_of[b] == 1)
                def _():
                    kv_copies(b, block, c - 2**b)[n].wait_recv()

        arrived(0)
        joined = []
        for g in range(groups):
            tops, sums, _ = partial[g]
            keys = gathered(k_all, far, g)
            scores = scored(g, block, keys)
            weights, factors, totals = [], [], []
            for j in range(per_group):
                bits = masks[g * per_group + j, block]
                pieces = [
                    biased(piece, bits, local_bits + b, bit_of[b])
                    for b, piece in enumerate(cut(scores, j, ctx_bits))
                ]
                top = jnp.maximum(tops[j], row_top(pieces))
                weight, total = raised(pieces, top)
                factor = jnp.exp2((tops[j] - top) * (DH**-0.5 * LOG2_E))
                weights.append(weight)
                factors.append(factor)
                totals.append(sums[j] * factor + total)
            joined.append((weights, factors, totals))
        arrived(1)
        for g in range(groups):
            weighted = partial[g][2]
            weights, factors, totals = joined[g]
            values = gathered(v_all, far, g)
            added = jnp.dot(
                jnp.concatenate(weights, axis=0), values, preferred_element_type=jnp.float32
            )
            for j in range(per_group):
                lines = slice(j * BLOCK, (j + 1) * BLOCK)
                ready[step, :, pl.ds((g * per_group + j) * DH, DH)] = (
                    (weighted[lines] * factors[j] + added[lines]) / totals[j]
                ).astype(jnp.bfloat16)

    def att_copy(step, owner, source_head, place):
        return pltpu.make_async_remote_copy(
            src_ref=ready.at[step],
            dst_ref=out.at[rows_of(place), pl.ds(pl.multiple_of(source_head * width, width), width)],
            send_sem=att_send.at[step],
            recv_sem=att_recv.at[source_head, place],
            device_id=(c, owner),
            device_id_type=MESH,
        )

    def own_copy(step):
        return pltpu.make_async_copy(
            ready.at[step],
            out.at[rows_of(step - others), pl.ds(pl.multiple_of(h * width, width), width)],
            own_sem.at[step - others],
        )

    def compute_step(step, carry):
        owner, place, block = block_at(step)
        attend(block, step)

        @pl.when(step < others)
        def _():
            att_copy(step, owner, h, place).start()

        @pl.when(step >= others)
        def _():
            own_copy(step).start()

        return carry

    lax.fori_loop(0, blocks, compute_step, 0)

    for place in range(per_owner):
        own_copy(others + place).wait()
        for d in range(1, nh):
            source_head = (h + d) % nh
            att_copy(0, source_head, source_head, place).wait_recv()

    def drain(step, carry):
        owner, place, block = block_at(step)
        for b in range(ctx_bits):

            @pl.when(bit_of[b] == 0)
            def _():
                for copy in kv_copies(b, block, c + 2**b):
                    copy.wait_send()

        @pl.when(step < others)
        def _():
            att_copy(step, owner, h, place).wait_send()

        return carry

    lax.fori_loop(0, blocks, drain, 0)


def norm_kernel(residual, attended, gain, stream, normed):
    summed = residual[...].astype(jnp.float32) + attended[...].astype(jnp.float32)
    stream[...] = summed.astype(jnp.bfloat16)
    mean = jnp.mean(summed * summed, axis=-1, keepdims=True)
    normed[...] = (
        summed * lax.rsqrt(mean + EPSILON) * gain[...].astype(jnp.float32)[None, :]
    ).astype(jnp.bfloat16)


def shards(queries, keys, values, block_masks, residual, norm_gain):
    tokens, width = queries.shape
    kv_width = keys.shape[1]
    blocks = tokens // BLOCK
    groups = kv_width // DH
    per_group = width // kv_width
    nh = lax.axis_size("head")
    ctx_bits = lax.axis_size("ctx").bit_length() - 1
    rows, full = residual.shape
    per_owner = rows // BLOCK
    sizes = (ctx_bits, nh, groups, per_group, blocks, per_owner)
    in_hbm = pl.BlockSpec(memory_space=pltpu.HBM)
    attended = pl.pallas_call(
        functools.partial(attention_kernel, sizes),
        out_shape=jax.ShapeDtypeStruct((rows, full), jnp.bfloat16),
        in_specs=[in_hbm] * 4,
        out_specs=in_hbm,
        scratch_shapes=[
            pltpu.SMEM(block_masks.shape, jnp.int32),
            pltpu.VMEM((tokens, width), jnp.bfloat16),
            pltpu.VMEM((1 + ctx_bits, tokens, kv_width), jnp.bfloat16),
            pltpu.VMEM((1 + ctx_bits, tokens, kv_width), jnp.bfloat16),
            pltpu.VMEM((blocks, BLOCK, width), jnp.bfloat16),
            pltpu.SemaphoreType.DMA((4,)),
            pltpu.SemaphoreType.DMA((2, ctx_bits, blocks)),
            pltpu.SemaphoreType.DMA((2, ctx_bits, blocks)),
            pltpu.SemaphoreType.DMA((blocks,)),
            pltpu.SemaphoreType.DMA((nh, per_owner)),
            pltpu.SemaphoreType.DMA((per_owner,)),
        ],
        compiler_params=pltpu.CompilerParams(
            collective_id=0, has_side_effects=True, vmem_limit_bytes=48 * 2**20
        ),
        name="attention",
    )(*(pltpu.with_memory_space_constraint(x, pltpu.HBM) for x in (block_masks, queries, keys, values)))
    tile = min(rows, 128)
    by_rows = pl.BlockSpec((tile, full), lambda n: (n, 0))
    return pl.pallas_call(
        norm_kernel,
        grid=(rows // tile,),
        out_shape=(jax.ShapeDtypeStruct((rows, full), jnp.bfloat16),) * 2,
        in_specs=[by_rows, by_rows, pl.BlockSpec((full,), lambda n: (0,))],
        out_specs=(by_rows, by_rows),
        compiler_params=pltpu.CompilerParams(vmem_limit_bytes=32 * 2**20),
        name="add_norm",
    )(residual, attended, norm_gain)


def solution(mesh):
    in_specs = (
        P("ctx", "head"),
        P("ctx", "head"),
        P("ctx", "head"),
        P("head", "ctx"),
        P(("ctx", "head"), None),
        P(),
    )
    out_specs = (P(("ctx", "head"), None), P(("ctx", "head"), None))
    return jax.shard_map(shards, mesh=mesh, in_specs=in_specs, out_specs=out_specs, check_vma=False)
```
